32 devices in a mesh: row: 8 (over z, y), col: 4 (over x, core).
Axes of the slice: x: 2, y: 2, z: 4, core: 2. Of those that a mesh axis runs over, the one named last changes fastest.
Arguments:
- lesser: bfloat16 [4096, 4096], P('row', 'col'), may hold values from -6 to 6
- greater: bfloat16 [4096, 4096], P('row', 'col'), may hold values from -6 to 6
- screened_lesser: bfloat16 [4096, 4096], P('row', 'col'), may hold values from -6 to 6
- screened_greater: bfloat16 [4096, 4096], P('row', 'col'), may hold values from -6 to 6
Outputs:
- collision: float32 [4096, 1024], P('row', 'col')
The draws below stay inside these ranges and needn't reach their ends.
All inputs are finite; a program needn't handle non-finite values.
Results may differ from the reference program's by a relative error of at most 0.0051.
Values may be sent and summed in bfloat16 or wider, within the bound.
No kernel may reach another device: no remote copies, remote signals or barrier semaphores. Data moves between devices by JAX's collectives and lax.ppermute only.
A program may use at most 64 MiB of HBM per device.

```python
import jax
import jax.numpy as jnp
from jax import lax

TILE_ORDER = 1024
WINDOW = 256
SLAB_ORDER = 4096
ROWS_DEV = 512
N_ROW = 8
N_COL = 4


def levels(rng, dims, pieces, low, largest):
    level = 1.0
    for position, blocks in pieces:
        draws = jax.random.uniform(jax.random.fold_in(jax.random.fold_in(rng, 6), position), (blocks,), jnp.float32, low / len(pieces), largest / len(pieces))
        level = level * jnp.repeat(jnp.exp(draws), dims[position] // blocks).reshape((-1,) + (1,) * (len(dims) - 1 - position))
    return level


def gaussian(stream_key, dims, scale, limit, split=(), held_as=jnp.bfloat16):
    level = levels(stream_key, dims, split, -0.22, 0.18) if split else 1.0
    values = jax.random.normal(stream_key, dims, jnp.float32) * scale * level
    return jnp.minimum(jnp.maximum(values, -limit), limit).astype(held_as)


def setup_inputs(seed: int = 0) -> dict:
    streams_of = jax.random.split(jax.random.key(seed), 5)
    lesser = gaussian(streams_of[0], (SLAB_ORDER, SLAB_ORDER), 1.0, 6.0, ((0, 8), (1, 4)))
    greater = gaussian(streams_of[1], (SLAB_ORDER, SLAB_ORDER), 1.0, 6.0, ((0, 8), (1, 4)))
    screened_lesser = gaussian(streams_of[2], (SLAB_ORDER, SLAB_ORDER), 1.0, 6.0, ((0, 8), (1, 4)))
    screened_greater = gaussian(streams_of[3], (SLAB_ORDER, SLAB_ORDER), 1.0, 6.0, ((0, 8), (1, 4)))
    return {"lesser": lesser, "greater": greater, "screened_lesser": screened_lesser, "screened_greater": screened_greater}


def reference(lesser, greater, screened_lesser, screened_greater):
    slab = lesser.shape[0]
    scale = float(slab) ** -0.5

    def one_block(block):
        start = (block * ROWS_DEV).astype(jnp.int32)
        zero = jnp.zeros((), jnp.int32)
        less_rows = lax.dynamic_slice(lesser, (start, zero), (ROWS_DEV, slab)).astype(jnp.float32)
        great_rows = lax.dynamic_slice(greater, (start, zero), (ROWS_DEV, slab)).astype(jnp.float32)
        wless_rows = lax.dynamic_slice(screened_lesser, (start, zero), (ROWS_DEV, slab)).astype(jnp.float32)
        wgreat_rows = lax.dynamic_slice(screened_greater, (start, zero), (ROWS_DEV, slab)).astype(jnp.float32)
        prod_less = less_rows * wless_rows
        prod_great = great_rows * wgreat_rows
        sigma_less = prod_less.astype(jnp.bfloat16)
        later = start + jnp.arange(ROWS_DEV, dtype=jnp.int32)
        inner = jnp.arange(slab, dtype=jnp.int32)
        sigma_ret = jnp.where(inner[None, :] <= later[:, None], prod_great - prod_less, 0.0).astype(jnp.bfloat16)
        green_win = lax.dynamic_slice(lesser, (zero, start), (slab, WINDOW))
        great_win = lax.dynamic_slice(greater, (zero, start), (slab, WINDOW))
        diff_win = (green_win.astype(jnp.float32) - great_win.astype(jnp.float32)).astype(jnp.bfloat16)
        window_times = start + jnp.arange(WINDOW, dtype=jnp.int32)
        diff_win = jnp.where(inner[:, None] <= window_times[None, :], diff_win, jnp.zeros((), jnp.bfloat16))
        ret_tiles = sigma_ret.reshape(ROWS_DEV, N_COL, TILE_ORDER).astype(jnp.float32)
        less_tiles = sigma_less.reshape(ROWS_DEV, N_COL, TILE_ORDER).astype(jnp.float32)
        green_tiles = green_win.reshape(N_COL, TILE_ORDER, WINDOW).astype(jnp.float32)
        diff_tiles = diff_win.reshape(N_COL, TILE_ORDER, WINDOW).astype(jnp.float32)
        partial_value = jnp.einsum("tcu,cuw->tcw", ret_tiles, green_tiles) + jnp.einsum("tcu,cuw->tcw", less_tiles, diff_tiles)
        partial_value = scale * partial_value
        return jnp.cumsum(partial_value, axis=1).reshape(ROWS_DEV, N_COL * WINDOW)

    blocks = lax.map(one_block, jnp.arange(N_ROW, dtype=jnp.int32))
    return blocks.reshape(N_ROW * ROWS_DEV, N_COL * WINDOW)
```

```python
import functools

import jax
import jax.numpy as jnp
from jax import lax
from jax.experimental import pallas as pl
from jax.experimental.pallas import tpu as pltpu
from jax.sharding import PartitionSpec as P

WINDOW = 256
LANES = 128
AXES = ("row", "col")
BF16 = jnp.bfloat16
F32 = jnp.float32
ROOM = pltpu.CompilerParams(vmem_limit_bytes=16 * 2**20)


def routes(row_devices, col_devices):
    ratio = row_devices // col_devices
    half = col_devices // 2

    def at(z, y, g):
        return (z * ratio + y) * col_devices + g

    first = [
        (at(z, y, g), at(z, y, g - half)) for z in range(half) for y in range(ratio) for g in range(half, col_devices)
    ]
    near, far, second = [], [], []
    for s in range(ratio):
        near.append([])
        far.append([])
        second.append([])
        for z in range(col_devices):
            for y in range(ratio):
                to = (y + s) % ratio
                for g in range(z, col_devices):
                    if z < half <= g:
                        far[s].append((at(z, y, g), at(g, to, z)))
                        second[s].append((at(z, y, g - half), at(g, to, z)))
                    elif z < g or y < to:
                        near[s].append((at(z, y, g), at(g, to, z)))
    later, d = [], 1
    while d < col_devices:
        d *= 2
    for d in [*range(2, d), 1][: d - 1]:
        pairs = []
        for z in range(col_devices):
            for y in range(ratio):
                for c in range(z + 1):
                    if c < c ^ d < col_devices:
                        pairs.append((at(z, y, c), at(z, y, c ^ d)))
        later.append(pairs)
    return near, far, first, second, later


def held(shape, dtype):
    return pltpu.VMEM(shape, dtype)


def keep(x):
    return pltpu.with_memory_space_constraint(x, pltpu.VMEM)


def place():
    return lax.axis_index("row"), lax.axis_index("col")


def copies(jobs, sem):
    out = [pltpu.make_async_copy(src, dst, sem.at[i]) for i, (src, dst) in enumerate(jobs)]
    for copy in out:
        copy.start()
    for copy in out:
        copy.wait()


def pack(lesser, greater, spans):
    rows, width = lesser.shape
    ratio = width // rows

    def kernel(less_ref, great_ref, *refs):
        outs, sem = refs[:-1], refs[-1]
        my_row, _ = place()
        jobs = []
        for out, (s, r0, r1, c0, c1) in zip(outs, spans):
            block = lax.rem(my_row + s, ratio)
            start = pl.multiple_of(block * rows + c0, LANES)
            for i, ref in enumerate((less_ref, great_ref)):
                jobs.append((ref.at[pl.ds(r0, r1 - r0), pl.ds(start, c1 - c0)], out.at[i]))
        copies(jobs, sem)

    return pl.pallas_call(
        kernel,
        out_shape=[held((2, r1 - r0, c1 - c0), BF16) for _, r0, r1, c0, c1 in spans],
        in_specs=[pl.BlockSpec(memory_space=pl.ANY)] * 2,
        out_specs=[pl.BlockSpec(memory_space=pltpu.VMEM)] * len(spans),
        scratch_shapes=[pltpu.SemaphoreType.DMA((2 * len(spans),))],
        compiler_params=ROOM,
        name="pack_windows",
    )(lesser, greater)


def sigmas(lesser, greater, screened_lesser, screened_greater):
    rows, width = lesser.shape
    ratio = width // rows
    tile = rows // 2

    def kernel(less_ref, great_ref, wless_ref, wgreat_ref, ret_ref, out_ref):
        my_row, my_col = place()
        k, i = pl.program_id(0), pl.program_id(1)
        prod_less = less_ref[...].astype(F32) * wless_ref[...].astype(F32)
        prod_great = great_ref[...].astype(F32) * wgreat_ref[...].astype(F32)
        later = my_row * rows + i * tile + lax.broadcasted_iota(jnp.int32, (tile, rows), 0)
        inner = my_col * width + k * rows + lax.broadcasted_iota(jnp.int32, (tile, rows), 1)
        ret_ref[0] = jnp.where(inner <= later, prod_great - prod_less, 0.0).astype(BF16)
        out_ref[0] = prod_less.astype(BF16)

    return pl.pallas_call(
        kernel,
        grid=(ratio, rows // tile),
        out_shape=[held((ratio, rows, rows), BF16)] * 2,
        in_specs=[pl.BlockSpec((tile, rows), lambda k, i: (i, k))] * 4,
        out_specs=[pl.BlockSpec((1, tile, rows), lambda k, i: (k, i, 0))] * 2,
        compiler_params=ROOM,
        name="sigma_blocks",
    )(lesser, greater, screened_lesser, screened_greater)


def block_term(ret_ref, less_ref, k, win, my_row, my_col, rows, width, first):
    green, great = win(0), win(1)
    diff = (green.astype(F32) - great.astype(F32)).astype(BF16)
    inner = my_col * width + k * rows + lax.broadcasted_iota(jnp.int32, diff.shape, 0)
    times = my_row * rows + first + lax.broadcasted_iota(jnp.int32, diff.shape, 1)
    diff = jnp.where(inner <= times, diff, jnp.zeros((), BF16))
    return jnp.dot(ret_ref[k], green, preferred_element_type=F32) + jnp.dot(
        less_ref[k], diff, preferred_element_type=F32
    )


def partial(ret, less, own, wins, first, cols, width, scale):
    ratio, rows, _ = ret.shape
    counts = [len(pieces) for pieces in wins]

    def kernel(ret_ref, less_ref, own_ref, *refs):
        out_ref, send_ref = refs[-2:]
        my_row, my_col = place()
        total, at = None, 0
        for s in range(ratio):
            k = lax.rem(my_row + ratio - s, ratio)
            mine = refs[at : at + counts[s]]
            at += counts[s]

            def win(i, s=s, mine=mine):
                got = None
                for (start, _), ref in zip(wins[s], mine):
                    piece = ref[i, :, start : start + cols]
                    got = piece if got is None else got + piece
                if s == 0:
                    got = jnp.where(my_col == my_row // ratio, own_ref[i], got)
                return got

            term = block_term(ret_ref, less_ref, k, win, my_row, my_col, rows, width, first)
            total = term if total is None else total + term
        total = scale * total
        out_ref[...] = total
        send_ref[...] = total.astype(BF16)

    return pl.pallas_call(
        kernel,
        out_shape=[held((rows, cols), F32), held((rows, cols), BF16)],
        in_specs=[pl.BlockSpec(memory_space=pltpu.VMEM)] * (3 + sum(counts)),
        out_specs=[pl.BlockSpec(memory_space=pltpu.VMEM)] * 2,
        compiler_params=ROOM,
        name="partial",
    )(*map(keep, [ret, less, own]), *[keep(x) for pieces in wins for _, x in pieces])


def accumulate(parts, got):
    rows, cols = parts[0].shape
    n = len(parts)

    def kernel(*refs):
        part_refs, out_ref = refs[:n], refs[-1]
        got_refs = refs[n:-1]
        each = len(got_refs) // n
        for q in range(n):
            total = part_refs[q][...]
            for ref in got_refs[q * each : (q + 1) * each]:
                total = total + ref[...].astype(F32)
            out_ref[:, q * cols : (q + 1) * cols] = total

    return pl.pallas_call(
        kernel,
        out_shape=jax.ShapeDtypeStruct((rows, n * cols), F32),
        in_specs=[pl.BlockSpec(memory_space=pltpu.VMEM)] * (n + sum(map(len, got))),
        out_specs=pl.BlockSpec(memory_space=pltpu.VMEM),
        compiler_params=ROOM,
        name="accumulate",
    )(*map(keep, parts), *[keep(g) for group in got for g in group])


def local(lesser, greater, screened_lesser, screened_greater):
    rows, width = lesser.shape
    row_devices, col_devices = lax.axis_size("row"), lax.axis_size("col")
    ratio = row_devices // col_devices
    scale = float(width * col_devices) ** (-0.5)
    near, far, first, second, later = routes(row_devices, col_devices)
    chunks = WINDOW // LANES

    def send(x, pairs):
        return lax.ppermute(x, AXES, pairs)

    jobs = [(s, q) for q in range(chunks) for s in reversed(range(ratio))]
    spans = [(s, 0, rows, q * LANES, (q + 1) * LANES) for s, q in jobs]
    odd = range(1, ratio, 2)
    spans += [(s, 0, rows, 0, WINDOW) for s in odd]
    packed = pack(lesser, greater, spans)
    ready = dict(zip(jobs, packed))
    wins, hops = {}, {}
    for s, q in jobs:
        if s % 2:
            hops[s, q] = send(ready[s, q], first)
        else:
            wins[s, q] = [(0, send(ready[s, q], near[s] + far[s]))]
    beside = {s: send(x, near[s]) for s, x in zip(odd, packed[len(jobs) :])}
    for s, q in jobs:
        if s % 2:
            wins[s, q] = [(0, send(hops[s, q], second[s])), (q * LANES, beside[s])]
    ret, less = sigmas(lesser, greater, screened_lesser, screened_greater)
    parts, got = [], []
    for q in range(chunks):
        mine = [wins[s, q] for s in range(ratio)]
        part, out = partial(ret, less, ready[0, q], mine, q * LANES, LANES, width, scale)
        parts.append(part)
        got.append([send(out, pairs) for pairs in later])
    return accumulate(parts, got)


def solution(mesh):
    in_specs = (P("row", "col"),) * 4
    return jax.shard_map(local, mesh=mesh, in_specs=in_specs, out_specs=P("row", "col"), check_vma=False)
```

```python
import functools

import jax
import jax.numpy as jnp
from jax import lax
from jax.experimental import pallas as pl
from jax.experimental.pallas import tpu as pltpu
from jax.sharding import PartitionSpec as P

WINDOW = 256
LANES = 128
AXES = ("row", "col")
BF16 = jnp.bfloat16
F32 = jnp.float32
ROOM = pltpu.CompilerParams(vmem_limit_bytes=16 * 2**20)


def routes(row_devices, col_devices):
    ratio = row_devices // col_devices
    half = col_devices // 2
    straight = col_devices - half // 2

    def at(z, y, g):
        return (z * ratio + y) * col_devices + g

    plan = []
    for s in range(ratio):
        first, second, left = [], [], []
        near, hops = {}, []
        for z in range(col_devices):
            for y in range(ratio):
                to = (y + s) % ratio
                for g in range(z, col_devices):
                    src, dst = at(z, y, g), at(g, to, z)
                    if z < half and g >= straight:
                        hops.append((z, y, src, dst))
                    elif z < half <= g:
                        first.append((src, dst))
                    elif z < g or y < to:
                        near[dst] = src
        relays, kept = set(), set()
        for z, y, src, dst in hops:
            choice = None
            for g in range(half):
                relay = at(z, y, g)
                if relay in relays or relay in kept:
                    continue
                if relay not in near:
                    choice = relay
                    break
                if choice is None and near[relay] not in relays:
                    choice = relay
            if choice is None:
                left.append((src, dst))
                continue
            relays.add(choice)
            if choice in near:
                kept.add(near[choice])
            first.append((src, choice))
            second.append((choice, dst))
        for dst, src in near.items():
            if dst not in relays and src not in kept:
                first.append((src, dst))
            elif dst in relays and src in kept and (src, src) not in first:
                first.append((src, src))
                second.append((src, dst))
            else:
                left.append((src, dst))
        brings = {dst for src, dst in first if src != dst and dst not in relays}
        plan.append((first, second, left, brings))
    later, d = [], 1
    while d < col_devices:
        d *= 2
    for d in [*range(2, d), 1][: d - 1]:
        pairs = []
        for z in range(col_devices):
            for y in range(ratio):
                for c in range(z + 1):
                    if c < c ^ d < col_devices:
                        pairs.append((at(z, y, c), at(z, y, c ^ d)))
        later.append(pairs)
    return plan, later


def member(devices, index):
    found = jnp.int32(0)
    for word in range(max(devices, default=0) // 31 + 1):
        bits = sum(1 << (d % 31) for d in devices if d // 31 == word)
        found = found + jnp.where(index // 31 == word, (jnp.int32(bits) >> (index % 31)) & 1, 0)
    return found != 0


def held(shape, dtype):
    return pltpu.VMEM(shape, dtype)


def keep(x):
    return pltpu.with_memory_space_constraint(x, pltpu.VMEM)


def place():
    return lax.axis_index("row"), lax.axis_index("col")


def copies(jobs, sem):
    out = [pltpu.make_async_copy(src, dst, sem.at[i]) for i, (src, dst) in enumerate(jobs)]
    for copy in out:
        copy.start()
    for copy in out:
        copy.wait()


def pack(lesser, greater, spans):
    rows, width = lesser.shape
    ratio = width // rows

    def kernel(less_ref, great_ref, *refs):
        outs, sem = refs[:-1], refs[-1]
        my_row, _ = place()
        jobs = []
        for out, (s, r0, r1, c0, c1) in zip(outs, spans):
            block = lax.rem(my_row + s, ratio)
            start = pl.multiple_of(block * rows + c0, LANES)
            for i, ref in enumerate((less_ref, great_ref)):
                jobs.append((ref.at[pl.ds(r0, r1 - r0), pl.ds(start, c1 - c0)], out.at[i]))
        copies(jobs, sem)

    return pl.pallas_call(
        kernel,
        out_shape=[held((2, r1 - r0, c1 - c0), BF16) for _, r0, r1, c0, c1 in spans],
        in_specs=[pl.BlockSpec(memory_space=pl.ANY)] * 2,
        out_specs=[pl.BlockSpec(memory_space=pltpu.VMEM)] * len(spans),
        scratch_shapes=[pltpu.SemaphoreType.DMA((2 * len(spans),))],
        compiler_params=ROOM,
        name="pack_windows",
    )(*(pltpu.with_memory_space_constraint(x, pltpu.HBM) for x in (lesser, greater)))


def sigmas(lesser, greater, screened_lesser, screened_greater):
    rows, width = lesser.shape
    ratio = width // rows
    steps = 4
    tile = rows // steps

    def kernel(*refs):
        ins, (ret_ref, out_ref), bufs, sem = refs[:4], refs[4:6], refs[6:10], refs[10]
        my_row, my_col = place()
        loads = []
        for i in range(steps):
            at = pl.ds(i * tile, tile)
            loads.append([])
            for n in range(4):
                copy = pltpu.make_async_copy(ins[n].at[at], bufs[n].at[at], sem.at[4 * i + n])
                copy.start()
                loads[i].append(copy)
        for i in range(steps):
            for copy in loads[i]:
                copy.wait()
            at = pl.ds(i * tile, tile)
            for k in range(ratio):
                cols = pl.ds(k * rows, rows)
                less, great, wless, wgreat = (buf[at, cols].astype(F32) for buf in bufs)
                prod_less = less * wless
                later = my_row * rows + i * tile + lax.broadcasted_iota(jnp.int32, (tile, rows), 0)
                inner = my_col * width + k * rows + lax.broadcasted_iota(jnp.int32, (tile, rows), 1)
                ret_ref[k, at] = jnp.where(inner <= later, great * wgreat - prod_less, 0.0).astype(BF16)
                out_ref[k, at] = prod_less.astype(BF16)

    args = (lesser, greater, screened_lesser, screened_greater)
    return pl.pallas_call(
        kernel,
        out_shape=[held((ratio, rows, rows), BF16)] * 2,
        in_specs=[pl.BlockSpec(memory_space=pl.ANY)] * 4,
        out_specs=[pl.BlockSpec(memory_space=pltpu.VMEM)] * 2,
        scratch_shapes=[pltpu.VMEM((rows, width), BF16)] * 4 + [pltpu.SemaphoreType.DMA((4 * steps,))],
        compiler_params=ROOM,
        name="sigma_blocks",
    )(*(pltpu.with_memory_space_constraint(x, pltpu.HBM) for x in args))


def block_term(ret_ref, less_ref, k, win, my_row, my_col, rows, width, first):
    green, great = win(0), win(1)
    diff = (green.astype(F32) - great.astype(F32)).astype(BF16)
    inner = my_col * width + k * rows + lax.broadcasted_iota(jnp.int32, diff.shape, 0)
    times = my_row * rows + first + lax.broadcasted_iota(jnp.int32, diff.shape, 1)
    diff = jnp.where(inner <= times, diff, jnp.zeros((), BF16))
    return jnp.dot(ret_ref[k], green, preferred_element_type=F32) + jnp.dot(
        less_ref[k], diff, preferred_element_type=F32
    )


def partial(ret, less, own, wins, brings, first, width, scale, sent=()):
    ratio, rows, _ = ret.shape
    cols = own.shape[-1]
    counts = [len(pieces) for pieces in wins]
    col_devices = lax.axis_size("col")

    def kernel(ret_ref, less_ref, own_ref, *refs):
        outs = refs[len(refs) - (3 if sent else 2) :]
        my_row, my_col = place()
        total, at = None, len(sent)
        for s in range(ratio):
            k = lax.rem(my_row + ratio - s, ratio)
            mine = refs[at : at + counts[s]]
            at += counts[s]
            valid = member(brings[s], my_row * col_devices + my_col)

            def win(i, s=s, mine=mine, valid=valid):
                got = jnp.where(valid, mine[0][i], jnp.zeros((), BF16))
                for ref in mine[1:]:
                    got = got + ref[i]
                if s == 0:
                    got = jnp.where(my_col == my_row // ratio, own_ref[i], got)
                return got

            term = block_term(ret_ref, less_ref, k, win, my_row, my_col, rows, width, first)
            total = term if total is None else total + term
        total = scale * total
        outs[0][...] = total
        outs[1][...] = total.astype(BF16)
        if sent:
            for n in range(len(sent)):
                outs[2][:, n * cols : (n + 1) * cols] = refs[n][...]
            outs[2][:, len(sent) * cols :] = total.astype(BF16)

    shapes = [held((rows, cols), F32), held((rows, cols), BF16)]
    if sent:
        shapes.append(held((rows, (1 + len(sent)) * cols), BF16))
    return pl.pallas_call(
        kernel,
        out_shape=shapes,
        in_specs=[pl.BlockSpec(memory_space=pltpu.VMEM)] * (3 + len(sent) + sum(counts)),
        out_specs=[pl.BlockSpec(memory_space=pltpu.VMEM)] * len(shapes),
        compiler_params=ROOM,
        name="partial",
    )(*map(keep, [ret, less, own, *sent]), *[keep(x) for pieces in wins for x in pieces])


def accumulate(parts, got, beside):
    rows, cols = parts[0].shape
    n = len(parts)
    each = len(got[0])

    def kernel(*refs):
        part_refs, got_refs, beside_refs, out_ref = refs[:n], refs[n : n + n * each], refs[n + n * each : -1], refs[-1]
        for q in range(n):
            here = slice(q * cols, (q + 1) * cols)
            total = part_refs[q][...]
            for ref in got_refs[q * each : (q + 1) * each]:
                total = total + ref[...].astype(F32)
            for ref in beside_refs:
                total = total + ref[:, here].astype(F32)
            out_ref[:, here] = total

    args = [*parts, *[g for group in got for g in group], *beside]
    return pl.pallas_call(
        kernel,
        out_shape=jax.ShapeDtypeStruct((rows, n * cols), F32),
        in_specs=[pl.BlockSpec(memory_space=pltpu.VMEM)] * len(args),
        out_specs=pl.BlockSpec(memory_space=pltpu.VMEM),
        compiler_params=ROOM,
        name="accumulate",
    )(*map(keep, args))


def local(lesser, greater, screened_lesser, screened_greater):
    rows, width = lesser.shape
    row_devices, col_devices = lax.axis_size("row"), lax.axis_size("col")
    ratio = row_devices // col_devices
    scale = float(width * col_devices) ** (-0.5)
    plan, later = routes(row_devices, col_devices)
    chunks = WINDOW // LANES

    def send(x, pairs):
        return lax.ppermute(x, AXES, pairs)

    jobs = [(s, q) for q in range(chunks) for s in range(ratio)]
    packed = pack(lesser, greater, [(s, 0, rows, q * LANES, (q + 1) * LANES) for s, q in jobs])
    ready = dict(zip(jobs, packed))
    hop = {(s, q): send(ready[s, q], plan[s][0]) for s, q in jobs}
    ret, less = sigmas(lesser, greater, screened_lesser, screened_greater)
    if ratio > 1:
        hop[0, 0], ret, less = lax.optimization_barrier((hop[0, 0], ret, less))
    wins = {(s, q): [hop[s, q], send(hop[s, q], plan[s][1])] for s, q in jobs}
    for s, q in jobs:
        if plan[s][2]:
            wins[s, q].append(send(ready[s, q], plan[s][2]))
    brings = [p[3] for p in plan]
    parts, sent, got = [], [], []
    for q in range(chunks):
        mine = [wins[s, q] for s in range(ratio)]
        last = q == chunks - 1
        part, out, *both = partial(
            ret, less, ready[0, q], mine, brings, q * LANES, width, scale, ()
        )
        parts.append(part)
        sent.append(out)
        got.append([send(out, pairs) for pairs in later])
    return accumulate(parts, got, [])


def solution(mesh):
    in_specs = (P("row", "col"),) * 4
    return jax.shard_map(local, mesh=mesh, in_specs=in_specs, out_specs=P("row", "col"), check_vma=False)
```

```python
import functools

import jax
import jax.numpy as jnp
from jax import lax
from jax.experimental import pallas as pl
from jax.experimental.pallas import tpu as pltpu
from jax.sharding import PartitionSpec as P

WINDOW = 256
LANES = 128
AXES = ("row", "col")
BF16 = jnp.bfloat16
F32 = jnp.float32
ROOM = pltpu.CompilerParams(vmem_limit_bytes=16 * 2**20)


def route(row_devices, col_devices, s, eased):
    ratio = row_devices // col_devices
    half = col_devices // 2
    straight = col_devices - half // 2

    def at(z, y, g):
        return (z * ratio + y) * col_devices + g

    first, second, left = [], [], []
    near, hops = {}, []
    for z in range(col_devices):
        for y in range(ratio):
            to = (y + s) % ratio
            for g in range(z, col_devices):
                src, dst = at(z, y, g), at(g, to, z)
                if z < half and g >= straight and not (eased and z % 2):
                    hops.append((z, y, src, dst))
                elif z < half <= g:
                    first.append((src, dst))
                elif z < g or y < to:
                    near[dst] = src
    relays, kept = set(), set()
    for z, y, src, dst in hops:
        choice = None
        for g in range(half):
            relay = at(z, y, g)
            if relay in relays or relay in kept:
                continue
            if relay not in near:
                choice = relay
                break
            if choice is None and near[relay] not in relays:
                choice = relay
        if choice is None:
            left.append((src, dst))
            continue
        relays.add(choice)
        if choice in near:
            kept.add(near[choice])
        first.append((src, choice))
        second.append((choice, dst))
    for dst, src in near.items():
        if dst not in relays and src not in kept:
            first.append((src, dst))
        elif dst in relays and src in kept and (src, src) not in first:
            first.append((src, src))
            second.append((src, dst))
        else:
            left.append((src, dst))
    brings = {dst for src, dst in first if src != dst and dst not in relays}
    return first, second, left, brings


def onward(row_devices, col_devices):
    ratio = row_devices // col_devices

    def at(z, y, c):
        return (z * ratio + y) * col_devices + c

    across = []
    for d in range(2, col_devices, 2):
        across.append([])
        for z in range(col_devices):
            for y in range(ratio):
                for c in range(min(z + 1, col_devices - d)):
                    across[-1].append((at(z, y, c), at(z, y, c + d)))
    along = []
    for z in range(col_devices):
        for y in range(ratio):
            for c in range(0, col_devices, 2):
                along.append((at(z, y, c), at(z, y, c + 1)))
                if c and z:
                    along.append((at(z, y, c + 1), at(z, y, c)))
    return across, along


def member(devices, index):
    found = jnp.int32(0)
    for word in range(max(devices, default=0) // 31 + 1):
        bits = sum(1 << (d % 31) for d in devices if d // 31 == word)
        found = found + jnp.where(index // 31 == word, (jnp.int32(bits) >> (index % 31)) & 1, 0)
    return found != 0


def held(shape, dtype):
    return pltpu.VMEM(shape, dtype)


def keep(x):
    return pltpu.with_memory_space_constraint(x, pltpu.VMEM)


def place():
    return lax.axis_index("row"), lax.axis_index("col")


def copies(jobs, sem):
    out = [pltpu.make_async_copy(src, dst, sem.at[i]) for i, (src, dst) in enumerate(jobs)]
    for copy in out:
        copy.start()
    for copy in out:
        copy.wait()


def pack(lesser, greater, spans):
    rows, width = lesser.shape
    ratio = width // rows

    def kernel(less_ref, great_ref, *refs):
        outs, sem = refs[:-1], refs[-1]
        my_row, _ = place()
        jobs = []
        for out, (s, r0, r1, c0, c1) in zip(outs, spans):
            block = lax.rem(my_row + s, ratio)
            start = pl.multiple_of(block * rows + c0, LANES)
            for i, ref in enumerate((less_ref, great_ref)):
                jobs.append((ref.at[pl.ds(r0, r1 - r0), pl.ds(start, c1 - c0)], out.at[i]))
        copies(jobs, sem)

    return pl.pallas_call(
        kernel,
        out_shape=[held((2, r1 - r0, c1 - c0), BF16) for _, r0, r1, c0, c1 in spans],
        in_specs=[pl.BlockSpec(memory_space=pl.ANY)] * 2,
        out_specs=[pl.BlockSpec(memory_space=pltpu.VMEM)] * len(spans),
        scratch_shapes=[pltpu.SemaphoreType.DMA((2 * len(spans),))],
        compiler_params=ROOM,
        name="pack_windows",
    )(*(pltpu.with_memory_space_constraint(x, pltpu.HBM) for x in (lesser, greater)))


def sigmas(lesser, greater, screened_lesser, screened_greater):
    rows, width = lesser.shape
    ratio = width // rows
    steps = 4
    tile = rows // steps

    def kernel(*refs):
        ins, (ret_ref, out_ref), bufs, sem = refs[:4], refs[4:6], refs[6:10], refs[10]
        my_row, my_col = place()
        loads = []
        for i in range(steps):
            at = pl.ds(i * tile, tile)
            loads.append([])
            for n in range(4):
                copy = pltpu.make_async_copy(ins[n].at[at], bufs[n].at[at], sem.at[4 * i + n])
                copy.start()
                loads[i].append(copy)
        for i in range(steps):
            for copy in loads[i]:
                copy.wait()
            at = pl.ds(i * tile, tile)
            for k in range(ratio):
                cols = pl.ds(k * rows, rows)
                less, great, wless, wgreat = (buf[at, cols].astype(F32) for buf in bufs)
                prod_less = less * wless
                later = my_row * rows + i * tile + lax.broadcasted_iota(jnp.int32, (tile, rows), 0)
                inner = my_col * width + k * rows + lax.broadcasted_iota(jnp.int32, (tile, rows), 1)
                ret_ref[k, at] = jnp.where(inner <= later, great * wgreat - prod_less, 0.0).astype(BF16)
                out_ref[k, at] = prod_less.astype(BF16)

    args = (lesser, greater, screened_lesser, screened_greater)
    return pl.pallas_call(
        kernel,
        out_shape=[held((ratio, rows, rows), BF16)] * 2,
        in_specs=[pl.BlockSpec(memory_space=pl.ANY)] * 4,
        out_specs=[pl.BlockSpec(memory_space=pltpu.VMEM)] * 2,
        scratch_shapes=[pltpu.VMEM((rows, width), BF16)] * 4 + [pltpu.SemaphoreType.DMA((4 * steps,))],
        compiler_params=ROOM,
        name="sigma_blocks",
    )(*(pltpu.with_memory_space_constraint(x, pltpu.HBM) for x in args))


def block_term(ret_ref, less_ref, k, win, my_row, my_col, rows, width, first):
    green, great = win(0), win(1)
    diff = (green.astype(F32) - great.astype(F32)).astype(BF16)
    inner = my_col * width + k * rows + lax.broadcasted_iota(jnp.int32, diff.shape, 0)
    times = my_row * rows + first + lax.broadcasted_iota(jnp.int32, diff.shape, 1)
    diff = jnp.where(inner <= times, diff, jnp.zeros((), BF16))
    return jnp.dot(ret_ref[k], green, preferred_element_type=F32) + jnp.dot(
        less_ref[k], diff, preferred_element_type=F32
    )


def partial(ret, less, own, wins, brings, first, width, scale, sent=()):
    ratio, rows, _ = ret.shape
    cols = own.shape[-1]
    counts = [len(pieces) for pieces in wins]
    col_devices = lax.axis_size("col")

    def kernel(ret_ref, less_ref, own_ref, *refs):
        outs = refs[len(refs) - (3 if sent else 2) :]
        my_row, my_col = place()
        total, at = None, len(sent)
        for s in range(ratio):
            k = lax.rem(my_row + ratio - s, ratio)
            mine = refs[at : at + counts[s]]
            at += counts[s]
            valid = member(brings[s], my_row * col_devices + my_col)

            def win(i, s=s, mine=mine, valid=valid):
                got = jnp.where(valid, mine[0][i], jnp.zeros((), BF16))
                for ref in mine[1:]:
                    got = got + ref[i]
                if s == 0:
                    got = jnp.where(my_col == my_row // ratio, own_ref[i], got)
                return got

            term = block_term(ret_ref, less_ref, k, win, my_row, my_col, rows, width, first)
            total = term if total is None else total + term
        total = scale * total
        outs[0][...] = total
        outs[1][...] = total.astype(BF16)
        if sent:
            for n in range(len(sent)):
                outs[2][:, n * cols : (n + 1) * cols] = refs[n][...]
            outs[2][:, len(sent) * cols :] = total.astype(BF16)

    shapes = [held((rows, cols), F32), held((rows, cols), BF16)]
    if sent:
        shapes.append(held((rows, (1 + len(sent)) * cols), BF16))
    return pl.pallas_call(
        kernel,
        out_shape=shapes,
        in_specs=[pl.BlockSpec(memory_space=pltpu.VMEM)] * (3 + len(sent) + sum(counts)),
        out_specs=[pl.BlockSpec(memory_space=pltpu.VMEM)] * len(shapes),
        compiler_params=ROOM,
        name="partial",
    )(*map(keep, [ret, less, own, *sent]), *[keep(x) for pieces in wins for x in pieces])


def chunk_sums(before, part, got):
    rows, cols = part.shape
    start = before[0].shape[1] if before else 0

    def kernel(*refs):
        part_ref, got_refs, (total_ref, message_ref) = refs[0], refs[1 : 1 + len(got)], refs[-2:]
        _, my_col = place()
        came = jnp.zeros((rows, cols), F32)
        for ref in got_refs:
            came = came + ref[...].astype(F32)
        total = came + part_ref[...]
        if start:
            total_ref[:, :start] = refs[-4][...]
            message_ref[:, :start] = refs[-3][...]
        total_ref[:, start:] = total
        message_ref[:, start:] = jnp.where(lax.rem(my_col, 2) == 0, total, came).astype(BF16)

    args = [part, *got, *before]
    return pl.pallas_call(
        kernel,
        out_shape=[held((rows, start + cols), F32), held((rows, start + cols), BF16)],
        in_specs=[pl.BlockSpec(memory_space=pltpu.VMEM)] * len(args),
        out_specs=[pl.BlockSpec(memory_space=pltpu.VMEM)] * 2,
        compiler_params=ROOM,
        name="chunk_sums",
    )(*map(keep, args))


def accumulate(total, came):
    def kernel(total_ref, came_ref, out_ref):
        out_ref[...] = total_ref[...] + came_ref[...].astype(F32)

    return pl.pallas_call(
        kernel,
        out_shape=jax.ShapeDtypeStruct(total.shape, F32),
        in_specs=[pl.BlockSpec(memory_space=pltpu.VMEM)] * 2,
        out_specs=pl.BlockSpec(memory_space=pltpu.VMEM),
        compiler_params=ROOM,
        name="accumulate",
    )(keep(total), keep(came))


def local(lesser, greater, screened_lesser, screened_greater):
    rows, width = lesser.shape
    row_devices, col_devices = lax.axis_size("row"), lax.axis_size("col")
    ratio = row_devices // col_devices
    scale = float(width * col_devices) ** (-0.5)
    across, along = onward(row_devices, col_devices)
    chunks = WINDOW // LANES

    def send(x, pairs):
        return lax.ppermute(x, AXES, pairs)

    jobs = [(s, q) for q in range(chunks) for s in reversed(range(ratio))]
    packed = pack(lesser, greater, [(s, 0, rows, q * LANES, (q + 1) * LANES) for s, q in jobs])
    ready = dict(zip(jobs, packed))
    plan = {job: route(row_devices, col_devices, job[0], n in ()) for n, job in enumerate(jobs)}

    def send(x, pairs):
        return lax.ppermute(x, AXES, pairs)

    hop = {(s, q): send(ready[s, q], plan[s, q][0]) for s, q in jobs}
    inputs = (lesser, greater, screened_lesser, screened_greater)
    tie = jobs[1 % len(jobs)]
    hop[tie], inputs = lax.optimization_barrier((hop[tie], inputs))
    ret, less = sigmas(*inputs)
    tie = jobs[2 % len(jobs)]
    hop[tie], ret, less = lax.optimization_barrier((hop[tie], ret, less))
    wins = {(s, q): [hop[s, q], send(hop[s, q], plan[s, q][1])] for s, q in jobs}
    for s, q in jobs:
        if plan[s, q][2]:
            wins[s, q].append(send(ready[s, q], plan[s, q][2]))
    sums = ()
    for q in range(chunks):
        mine = [wins[s, q] for s in range(ratio)]
        brings = [plan[s, q][3] for s in range(ratio)]
        part, out = partial(ret, less, ready[0, q], mine, brings, q * LANES, width, scale)
        sums = chunk_sums(sums, part, [send(out, pairs) for pairs in across])
    total, message = sums
    return accumulate(total, send(message, along))


def solution(mesh):
    in_specs = (P("row", "col"),) * 4
    return jax.shard_map(local, mesh=mesh, in_specs=in_specs, out_specs=P("row", "col"), check_vma=False)
```

```python
import functools

import jax
import jax.numpy as jnp
from jax import lax
from jax.experimental import pallas as pl
from jax.experimental.pallas import tpu as pltpu
from jax.sharding import PartitionSpec as P

WINDOW = 256
LANES = 128
AXES = ("row", "col")
BF16 = jnp.bfloat16
F32 = jnp.float32
ROOM = pltpu.CompilerParams(vmem_limit_bytes=16 * 2**20)


def route(row_devices, col_devices, s, eased):
    ratio = row_devices // col_devices
    half = col_devices // 2
    straight = col_devices - half // 2

    def at(z, y, g):
        return (z * ratio + y) * col_devices + g

    first, second, left = [], [], []
    near, hops = {}, []
    for z in range(col_devices):
        for y in range(ratio):
            to = (y + s) % ratio
            for g in range(z, col_devices):
                src, dst = at(z, y, g), at(g, to, z)
                if z < half and g >= straight and not (eased and z % 2):
                    hops.append((z, y, src, dst))
                elif z < half <= g:
                    first.append((src, dst))
                elif z < g or y < to:
                    near[dst] = src
    relays, kept = set(), set()
    for z, y, src, dst in hops:
        choice = None
        for g in range(half):
            relay = at(z, y, g)
            if relay in relays or relay in kept:
                continue
            if relay not in near:
                choice = relay
                break
            if choice is None and near[relay] not in relays:
                choice = relay
        if choice is None:
            left.append((src, dst))
            continue
        relays.add(choice)
        if choice in near:
            kept.add(near[choice])
        first.append((src, choice))
        second.append((choice, dst))
    for dst, src in near.items():
        if dst not in relays and src not in kept:
            first.append((src, dst))
        elif dst in relays and src in kept and (src, src) not in first:
            first.append((src, src))
            second.append((src, dst))
        else:
            left.append((src, dst))
    brings = {dst for src, dst in first if src != dst and dst not in relays}
    return first, second, left, brings


def onward(row_devices, col_devices):
    ratio = row_devices // col_devices

    def at(z, y, c):
        return (z * ratio + y) * col_devices + c

    rows = [(z, y) for z in range(col_devices) for y in range(ratio)]
    across, askew = [], []
    for d in range(2, col_devices, 2):
        sources = [(z, y, c) for z, y in rows for c in range(min(z + 1, col_devices - d))]
        across.append([(at(z, y, c), at(z, y, c + d)) for z, y, c in sources])
        askew.append([(at(z, y, c), at(z, y, (c + d) ^ 1)) for z, y, c in sources])
    beside = [(at(z, y, c), at(z, y, c + 1)) for z, y in rows for c in range(0, min(z + 1, col_devices), 2)]
    along = [(at(z, y, c), at(z, y, c + 1)) for z, y in rows for c in range(0, col_devices, 2)]
    along += [(at(z, y, c + 1), at(z, y, c)) for z, y in rows for c in range(2, col_devices, 2) if z]
    return across, askew, along, beside


def member(devices, index):
    found = jnp.int32(0)
    for word in range(max(devices, default=0) // 31 + 1):
        bits = sum(1 << (d % 31) for d in devices if d // 31 == word)
        found = found + jnp.where(index // 31 == word, (jnp.int32(bits) >> (index % 31)) & 1, 0)
    return found != 0


def held(shape, dtype):
    return pltpu.VMEM(shape, dtype)


def keep(x):
    return pltpu.with_memory_space_constraint(x, pltpu.VMEM)


def place():
    return lax.axis_index("row"), lax.axis_index("col")


def copies(jobs, sem):
    out = [pltpu.make_async_copy(src, dst, sem.at[i]) for i, (src, dst) in enumerate(jobs)]
    for copy in out:
        copy.start()
    for copy in out:
        copy.wait()


def pack(lesser, greater, spans):
    rows, width = lesser.shape
    ratio = width // rows

    def kernel(less_ref, great_ref, *refs):
        outs, sem = refs[:-1], refs[-1]
        my_row, _ = place()
        jobs = []
        for out, (s, r0, r1, c0, c1) in zip(outs, spans):
            block = lax.rem(my_row + s, ratio)
            start = pl.multiple_of(block * rows + c0, LANES)
            for i, ref in enumerate((less_ref, great_ref)):
                jobs.append((ref.at[pl.ds(r0, r1 - r0), pl.ds(start, c1 - c0)], out.at[i]))
        copies(jobs, sem)

    return pl.pallas_call(
        kernel,
        out_shape=[held((2, r1 - r0, c1 - c0), BF16) for _, r0, r1, c0, c1 in spans],
        in_specs=[pl.BlockSpec(memory_space=pl.ANY)] * 2,
        out_specs=[pl.BlockSpec(memory_space=pltpu.VMEM)] * len(spans),
        scratch_shapes=[pltpu.SemaphoreType.DMA((2 * len(spans),))],
        compiler_params=ROOM,
        name="pack_windows",
    )(*(pltpu.with_memory_space_constraint(x, pltpu.HBM) for x in (lesser, greater)))


def sigmas(lesser, greater, screened_lesser, screened_greater):
    rows, width = lesser.shape
    ratio = width // rows
    steps = 8
    tile = rows // steps

    def kernel(*refs):
        ins, both_ref, bufs, sem = refs[:4], refs[4], refs[5:9], refs[9]
        my_row, my_col = place()
        loads = []
        for i in range(steps):
            at = pl.ds(i * tile, tile)
            loads.append([])
            for n in range(4):
                copy = pltpu.make_async_copy(ins[n].at[at], bufs[n].at[at], sem.at[4 * i + n])
                copy.start()
                loads[i].append(copy)
        for i in range(steps):
            for copy in loads[i]:
                copy.wait()
            at = pl.ds(i * tile, tile)
            for k in range(ratio):
                cols = pl.ds(k * rows, rows)
                less, great, wless, wgreat = (buf[at, cols].astype(F32) for buf in bufs)
                prod_less = less * wless
                later = my_row * rows + i * tile + lax.broadcasted_iota(jnp.int32, (tile, rows), 0)
                inner = my_col * width + k * rows + lax.broadcasted_iota(jnp.int32, (tile, rows), 1)
                both_ref[k, at, :rows] = jnp.where(inner <= later, great * wgreat - prod_less, 0.0).astype(BF16)
                both_ref[k, at, rows:] = prod_less.astype(BF16)

    args = (lesser, greater, screened_lesser, screened_greater)
    return pl.pallas_call(
        kernel,
        out_shape=held((ratio, rows, 2 * rows), BF16),
        in_specs=[pl.BlockSpec(memory_space=pl.ANY)] * 4,
        out_specs=pl.BlockSpec(memory_space=pltpu.VMEM),
        scratch_shapes=[pltpu.VMEM((rows, width), BF16)] * 4 + [pltpu.SemaphoreType.DMA((4 * steps,))],
        compiler_params=ROOM,
        name="sigma_blocks",
    )(*(pltpu.with_memory_space_constraint(x, pltpu.HBM) for x in args))


def block_term(both_ref, k, win, my_row, my_col, rows, width, first):
    green, great = win(0), win(1)
    diff = (green.astype(F32) - great.astype(F32)).astype(BF16)
    inner = my_col * width + k * rows + lax.broadcasted_iota(jnp.int32, diff.shape, 0)
    times = my_row * rows + first + lax.broadcasted_iota(jnp.int32, diff.shape, 1)
    diff = jnp.where(inner <= times, diff, jnp.zeros((), BF16))
    return jnp.dot(both_ref[k], jnp.concatenate([green, diff], axis=0), preferred_element_type=F32)


def partial(both, own, wins, brings, first, width, scale, sent=()):
    ratio, rows, _ = both.shape
    cols = own.shape[-1]
    counts = [len(pieces) for pieces in wins]
    col_devices = lax.axis_size("col")

    def kernel(both_ref, own_ref, *refs):
        outs = refs[len(refs) - (3 if sent else 2) :]
        my_row, my_col = place()
        some = my_col <= my_row // ratio

        @pl.when(some)
        def _():
            total, at = None, len(sent)
            for s in range(ratio):
                k = lax.rem(my_row + ratio - s, ratio)
                mine = refs[at : at + counts[s]]
                at += counts[s]
                valid = member(brings[s], my_row * col_devices + my_col)

                def win(i, s=s, mine=mine, valid=valid):
                    got = jnp.where(valid, mine[0][i], jnp.zeros((), BF16))
                    for ref in mine[1:]:
                        got = got + ref[i]
                    if s == 0:
                        got = jnp.where(my_col == my_row // ratio, own_ref[i], got)
                    return got

                term = block_term(both_ref, k, win, my_row, my_col, rows, width, first)
                total = term if total is None else total + term
            total = scale * total
            outs[0][...] = total
            outs[1][...] = total.astype(BF16)
            if sent:
                for n in range(len(sent)):
                    outs[2][:, n * cols : (n + 1) * cols] = refs[n][...]
                outs[2][:, len(sent) * cols :] = total.astype(BF16)

        @pl.when(jnp.logical_not(some))
        def _():
            for ref in outs:
                ref[...] = jnp.zeros(ref.shape, ref.dtype)

    shapes = [held((rows, cols), F32), held((rows, cols), BF16)]
    if sent:
        shapes.append(held((rows, (1 + len(sent)) * cols), BF16))
    return pl.pallas_call(
        kernel,
        out_shape=shapes,
        in_specs=[pl.BlockSpec(memory_space=pltpu.VMEM)] * (2 + len(sent) + sum(counts)),
        out_specs=[pl.BlockSpec(memory_space=pltpu.VMEM)] * len(shapes),
        compiler_params=ROOM,
        name="partial",
    )(*map(keep, [both, own, *sent]), *[keep(x) for pieces in wins for x in pieces])


def chunk_sums(part, got):
    def kernel(part_ref, *refs):
        _, my_col = place()
        came = jnp.zeros(part_ref.shape, F32)
        for ref in refs[:-2]:
            came = came + ref[...].astype(F32)
        total = came + part_ref[...]
        refs[-2][...] = total
        refs[-1][...] = jnp.where(lax.rem(my_col, 2) == 0, total, came).astype(BF16)

    args = [part, *got]
    return pl.pallas_call(
        kernel,
        out_shape=[held(part.shape, F32), held(part.shape, BF16)],
        in_specs=[pl.BlockSpec(memory_space=pltpu.VMEM)] * len(args),
        out_specs=[pl.BlockSpec(memory_space=pltpu.VMEM)] * 2,
        compiler_params=ROOM,
        name="chunk_sums",
    )(*map(keep, args))


def accumulate(totals, came):
    rows, cols = totals[0].shape
    n = len(totals)

    def kernel(*refs):
        for q in range(n):
            refs[-1][:, q * cols : (q + 1) * cols] = refs[q][...] + refs[n + q][...].astype(F32)

    return pl.pallas_call(
        kernel,
        out_shape=jax.ShapeDtypeStruct((rows, n * cols), F32),
        in_specs=[pl.BlockSpec(memory_space=pltpu.VMEM)] * (2 * n),
        out_specs=pl.BlockSpec(memory_space=pltpu.VMEM),
        compiler_params=ROOM,
        name="accumulate",
    )(*map(keep, [*totals, *came]))


def local(lesser, greater, screened_lesser, screened_greater):
    rows, width = lesser.shape
    row_devices, col_devices = lax.axis_size("row"), lax.axis_size("col")
    ratio = row_devices // col_devices
    scale = float(width * col_devices) ** (-0.5)
    across, askew, along, beside = onward(row_devices, col_devices)
    chunks = WINDOW // LANES

    def send(x, pairs):
        return lax.ppermute(x, AXES, pairs)

    jobs = [(s, q) for q in range(chunks) for s in range(ratio)]
    packed = pack(lesser, greater, [(s, 0, rows, q * LANES, (q + 1) * LANES) for s, q in jobs])
    ready = dict(zip(jobs, packed))
    plan = {job: route(row_devices, col_devices, job[0], n in ()) for n, job in enumerate(jobs)}

    def send(x, pairs):
        return lax.ppermute(x, AXES, pairs)

    hop = {(s, q): send(ready[s, q], plan[s, q][0]) for s, q in jobs}
    inputs = (lesser, greater, screened_lesser, screened_greater)
    both = sigmas(*inputs)
    tie = jobs[3 % len(jobs)]
    hop[tie], both = lax.optimization_barrier((hop[tie], both))
    wins = {(s, q): [hop[s, q], send(hop[s, q], plan[s, q][1])] for s, q in jobs}
    for s, q in jobs:
        if plan[s, q][2]:
            wins[s, q].append(send(ready[s, q], plan[s, q][2]))
    totals, came = [], []
    for q in range(chunks):
        mine = [wins[s, q] for s in range(ratio)]
        brings = [plan[s, q][3] for s in range(ratio)]
        part, out = partial(both, ready[0, q], mine, brings, q * LANES, width, scale)
        if q < chunks - 1:
            total, message = chunk_sums(part, [send(out, pairs) for pairs in across])
            came.append(send(message, along))
        else:
            total, _ = chunk_sums(part, [send(out, pairs) for pairs in across + askew])
            came.append(send(out, beside))
        totals.append(total)
    return accumulate(totals, came)


def solution(mesh):
    in_specs = (P("row", "col"),) * 4
    return jax.shard_map(local, mesh=mesh, in_specs=in_specs, out_specs=P("row", "col"), check_vma=False)
```

```python
import functools

import jax
import jax.numpy as jnp
from jax import lax
from jax.experimental import pallas as pl
from jax.experimental.pallas import tpu as pltpu
from jax.sharding import PartitionSpec as P

WINDOW = 256
LANES = 128
AXES = ("row", "col")
BF16 = jnp.bfloat16
F32 = jnp.float32
ROOM = pltpu.CompilerParams(vmem_limit_bytes=16 * 2**20)


def route(row_devices, col_devices, s):
    ratio = row_devices // col_devices
    half = col_devices // 2
    straight = col_devices - half // 2

    def at(z, y, g):
        return (z * ratio + y) * col_devices + g

    first, second, left = [], [], []
    near, hops = {}, []
    for z in range(col_devices):
        for y in range(ratio):
            to = (y + s) % ratio
            for g in range(z, col_devices):
                src, dst = at(z, y, g), at(g, to, z)
                if z < half and g >= straight:
                    hops.append((z, y, src, dst))
                elif z < half <= g:
                    first.append((src, dst))
                elif z < g or y < to:
                    near[dst] = src
    relays, kept = set(), set()
    for z, y, src, dst in hops:
        choice = None
        for g in range(half):
            relay = at(z, y, g)
            if relay in relays or relay in kept:
                continue
            if relay not in near:
                choice = relay
                break
            if choice is None and near[relay] not in relays:
                choice = relay
        if choice is None:
            left.append((src, dst))
            continue
        relays.add(choice)
        if choice in near:
            kept.add(near[choice])
        first.append((src, choice))
        second.append((choice, dst))
    for dst, src in near.items():
        if dst not in relays and src not in kept:
            first.append((src, dst))
        elif dst in relays and src in kept and (src, src) not in first:
            first.append((src, src))
            second.append((src, dst))
        else:
            left.append((src, dst))
    brings = {dst for src, dst in first if src != dst and dst not in relays}
    return first, second, left, brings


def onward(row_devices, col_devices):
    ratio = row_devices // col_devices

    def at(z, y, c):
        return (z * ratio + y) * col_devices + c

    rows = [(z, y) for z in range(col_devices) for y in range(ratio)]
    across, askew = [], []
    for d in range(2, col_devices, 2):
        pairs = [
            (at(z, y, c), at(z, y, c + d), at(z, y, (c + d) ^ 1))
            for z, y in rows
            for c in range(min(z + 1, col_devices - d))
        ]
        swapped = {at(z, y, c) for z, y in rows if z < col_devices // 2 for c in range(col_devices)}
        across.append([(src, other if src in swapped else same) for src, same, other in pairs])
        askew.append([(src, same if src in swapped else other) for src, same, other in pairs])
    beside = [(at(z, y, c), at(z, y, c + 1)) for z, y in rows for c in range(0, min(z + 1, col_devices), 2)]
    along = [(at(z, y, c), at(z, y, c + 1)) for z, y in rows for c in range(0, col_devices, 2)]
    along += [(at(z, y, c + 1), at(z, y, c)) for z, y in rows for c in range(2, col_devices, 2)]
    return across, askew, along, beside


def member(devices, index):
    found = jnp.int32(0)
    for word in range(max(devices, default=0) // 31 + 1):
        bits = sum(1 << (d % 31) for d in devices if d // 31 == word)
        found = found + jnp.where(index // 31 == word, (jnp.int32(bits) >> (index % 31)) & 1, 0)
    return found != 0


def held(shape, dtype):
    return pltpu.VMEM(shape, dtype)


def keep(x):
    return pltpu.with_memory_space_constraint(x, pltpu.VMEM)


def place():
    return lax.axis_index("row"), lax.axis_index("col")


def copies(jobs, sem):
    out = [pltpu.make_async_copy(src, dst, sem.at[i]) for i, (src, dst) in enumerate(jobs)]
    for copy in out:
        copy.start()
    for copy in out:
        copy.wait()


def pack(lesser, greater, spans):
    rows, width = lesser.shape
    ratio = width // rows

    def kernel(less_ref, great_ref, *refs):
        outs, sem = refs[:-1], refs[-1]
        my_row, _ = place()
        jobs = []
        for out, (s, r0, r1, c0, c1) in zip(outs, spans):
            block = lax.rem(my_row + s, ratio)
            start = pl.multiple_of(block * rows + c0, LANES)
            for i, ref in enumerate((less_ref, great_ref)):
                jobs.append((ref.at[pl.ds(r0, r1 - r0), pl.ds(start, c1 - c0)], out.at[i]))
        copies(jobs, sem)

    return pl.pallas_call(
        kernel,
        out_shape=[held((2, r1 - r0, c1 - c0), BF16) for _, r0, r1, c0, c1 in spans],
        in_specs=[pl.BlockSpec(memory_space=pl.ANY)] * 2,
        out_specs=[pl.BlockSpec(memory_space=pltpu.VMEM)] * len(spans),
        scratch_shapes=[pltpu.SemaphoreType.DMA((2 * len(spans),))],
        compiler_params=ROOM,
        name="pack_windows",
    )(*(pltpu.with_memory_space_constraint(x, pltpu.HBM) for x in (lesser, greater)))


def sigmas(lesser, greater, screened_lesser, screened_greater):
    rows, width = lesser.shape
    ratio = width // rows
    steps = 4
    tile = rows // steps

    def kernel(*refs):
        ins, both_ref, bufs, sem = refs[:4], refs[4], refs[5:9], refs[9]
        my_row, my_col = place()
        loads = []
        for i in range(steps):
            at = pl.ds(i * tile, tile)
            loads.append([])
            for n in range(4):
                copy = pltpu.make_async_copy(ins[n].at[at], bufs[n].at[at], sem.at[4 * i + n])
                copy.start()
                loads[i].append(copy)
        for i in range(steps):
            for copy in loads[i]:
                copy.wait()
            at = pl.ds(i * tile, tile)
            for k in range(ratio):
                cols = pl.ds(k * rows, rows)
                less, great, wless, wgreat = (buf[at, cols].astype(F32) for buf in bufs)
                prod_less = less * wless
                later = my_row * rows + i * tile + lax.broadcasted_iota(jnp.int32, (tile, rows), 0)
                inner = my_col * width + k * rows + lax.broadcasted_iota(jnp.int32, (tile, rows), 1)
                both_ref[k, at, :rows] = jnp.where(inner <= later, great * wgreat - prod_less, 0.0).astype(BF16)
                both_ref[k, at, rows:] = prod_less.astype(BF16)

    args = (lesser, greater, screened_lesser, screened_greater)
    return pl.pallas_call(
        kernel,
        out_shape=held((ratio, rows, 2 * rows), BF16),
        in_specs=[pl.BlockSpec(memory_space=pl.ANY)] * 4,
        out_specs=pl.BlockSpec(memory_space=pltpu.VMEM),
        scratch_shapes=[pltpu.VMEM((rows, width), BF16)] * 4 + [pltpu.SemaphoreType.DMA((4 * steps,))],
        compiler_params=ROOM,
        name="sigma_blocks",
    )(*(pltpu.with_memory_space_constraint(x, pltpu.HBM) for x in args))


def block_term(both_ref, k, win, my_row, my_col, rows, width, first):
    green, great = win(0), win(1)
    diff = (green.astype(F32) - great.astype(F32)).astype(BF16)
    inner = my_col * width + k * rows + lax.broadcasted_iota(jnp.int32, diff.shape, 0)
    times = my_row * rows + first + lax.broadcasted_iota(jnp.int32, diff.shape, 1)
    diff = jnp.where(inner <= times, diff, jnp.zeros((), BF16))
    return jnp.dot(both_ref[k], jnp.concatenate([green, diff], axis=0), preferred_element_type=F32)


def partial(both, own, wins, brings, first, width, scale):
    ratio, rows, _ = both.shape
    cols = own.shape[-1]
    counts = [len(pieces) for pieces in wins]
    col_devices = lax.axis_size("col")

    def kernel(both_ref, own_ref, *refs):
        outs = refs[-2:]
        my_row, my_col = place()
        some = my_col <= my_row // ratio

        @pl.when(some)
        def _():
            total, at = None, 0
            for s in range(ratio):
                k = lax.rem(my_row + ratio - s, ratio)
                mine = refs[at : at + counts[s]]
                at += counts[s]
                valid = member(brings[s], my_row * col_devices + my_col)

                def win(i, s=s, mine=mine, valid=valid):
                    got = jnp.where(valid, mine[0][i], jnp.zeros((), BF16))
                    for ref in mine[1:]:
                        got = got + ref[i]
                    if s == 0:
                        got = jnp.where(my_col == my_row // ratio, own_ref[i], got)
                    return got

                term = block_term(both_ref, k, win, my_row, my_col, rows, width, first)
                total = term if total is None else total + term
            total = scale * total
            outs[0][...] = total
            outs[1][...] = total.astype(BF16)

        @pl.when(jnp.logical_not(some))
        def _():
            for ref in outs:
                ref[...] = jnp.zeros(ref.shape, ref.dtype)

    shapes = [held((rows, cols), F32), held((rows, cols), BF16)]
    return pl.pallas_call(
        kernel,
        out_shape=shapes,
        in_specs=[pl.BlockSpec(memory_space=pltpu.VMEM)] * (2 + sum(counts)),
        out_specs=[pl.BlockSpec(memory_space=pltpu.VMEM)] * len(shapes),
        compiler_params=ROOM,
        name="partial",
    )(*map(keep, [both, own]), *[keep(x) for pieces in wins for x in pieces])


def chunk_sums(part, got, relayed):
    outs = [held(part.shape, F32)] + ([held(part.shape, BF16)] if relayed else [])

    def kernel(part_ref, *refs):
        _, my_col = place()
        came = jnp.zeros(part_ref.shape, F32)
        for ref in refs[: len(got)]:
            came = came + ref[...].astype(F32)
        total = came + part_ref[...]
        refs[len(got)][...] = total
        if relayed:
            refs[-1][...] = jnp.where(lax.rem(my_col, 2) == 0, total, came).astype(BF16)

    args = [part, *got]
    return pl.pallas_call(
        kernel,
        out_shape=outs,
        in_specs=[pl.BlockSpec(memory_space=pltpu.VMEM)] * len(args),
        out_specs=[pl.BlockSpec(memory_space=pltpu.VMEM)] * len(outs),
        compiler_params=ROOM,
        name="chunk_sums",
    )(*map(keep, args))


def accumulate(totals, came):
    rows, cols = totals[0].shape
    n = len(totals)

    def kernel(*refs):
        for q in range(n):
            refs[-1][:, q * cols : (q + 1) * cols] = refs[q][...] + refs[n + q][...].astype(F32)

    return pl.pallas_call(
        kernel,
        out_shape=jax.ShapeDtypeStruct((rows, n * cols), F32),
        in_specs=[pl.BlockSpec(memory_space=pltpu.VMEM)] * (2 * n),
        out_specs=pl.BlockSpec(memory_space=pltpu.VMEM),
        compiler_params=ROOM,
        name="accumulate",
    )(*map(keep, [*totals, *came]))


def local(lesser, greater, screened_lesser, screened_greater):
    rows, width = lesser.shape
    row_devices, col_devices = lax.axis_size("row"), lax.axis_size("col")
    ratio = row_devices // col_devices
    scale = float(width * col_devices) ** (-0.5)
    across, askew, along, beside = onward(row_devices, col_devices)
    chunks = WINDOW // LANES

    jobs = [(s, q) for q in range(chunks) for s in range(ratio)]
    packed = pack(lesser, greater, [(s, 0, rows, q * LANES, (q + 1) * LANES) for s, q in jobs])
    ready = dict(zip(jobs, packed))
    plan = {job: route(row_devices, col_devices, job[0]) for job in jobs}

    def send(x, pairs):
        return lax.ppermute(x, AXES, pairs)

    hop = {(s, q): send(ready[s, q], plan[s, q][0]) for s, q in jobs}
    both = sigmas(lesser, greater, screened_lesser, screened_greater)
    tie = jobs[-ratio]
    hop[tie], both = lax.optimization_barrier((hop[tie], both))
    wins = {(s, q): [hop[s, q], send(hop[s, q], plan[s, q][1])] for s, q in jobs}
    for s, q in jobs:
        if plan[s, q][2]:
            wins[s, q].append(send(ready[s, q], plan[s, q][2]))
    totals, came = [], []
    for q in range(chunks):
        mine = [wins[s, q] for s in range(ratio)]
        brings = [plan[s, q][3] for s in range(ratio)]
        part, out = partial(both, ready[0, q], mine, brings, q * LANES, width, scale)
        if q < chunks - 1:
            total, message = chunk_sums(part, [send(out, pairs) for pairs in across], True)
            came.append(send(message, along))
        else:
            (total,) = chunk_sums(part, [send(out, pairs) for pairs in across + askew], False)
            came.append(send(out, beside))
        totals.append(total)
    return accumulate(totals, came)


def solution(mesh):
    in_specs = (P("row", "col"),) * 4
    return jax.shard_map(local, mesh=mesh, in_specs=in_specs, out_specs=P("row", "col"), check_vma=False)
```

```python
import functools

import jax
import jax.numpy as jnp
from jax import lax
from jax.experimental import pallas as pl
from jax.experimental.pallas import tpu as pltpu
from jax.sharding import PartitionSpec as P

WINDOW = 256
LANES = 128
AXES = ("row", "col")
BF16 = jnp.bfloat16
F32 = jnp.float32
ROOM = pltpu.CompilerParams(vmem_limit_bytes=16 * 2**20)


def route(row_devices, col_devices, s):
    ratio = row_devices // col_devices
    half = col_devices // 2
    straight = col_devices - half // 2

    def at(z, y, g):
        return (z * ratio + y) * col_devices + g

    first, second, left = [], [], []
    near, hops = {}, []
    for z in range(col_devices):
        for y in range(ratio):
            to = (y + s) % ratio
            for g in range(z, col_devices):
                src, dst = at(z, y, g), at(g, to, z)
                if z < half and g >= straight:
                    hops.append((z, y, src, dst))
                elif z < half <= g:
                    first.append((src, dst))
                elif z < g or y < to:
                    near[dst] = src
    relays, kept = set(), set()
    for z, y, src, dst in hops:
        choice = None
        for g in range(half):
            relay = at(z, y, g)
            if relay in relays or relay in kept:
                continue
            if relay not in near:
                choice = relay
                break
            if choice is None and near[relay] not in relays:
                choice = relay
        if choice is None:
            left.append((src, dst))
            continue
        relays.add(choice)
        if choice in near:
            kept.add(near[choice])
        first.append((src, choice))
        second.append((choice, dst))
    for dst, src in near.items():
        if dst not in relays and src not in kept:
            first.append((src, dst))
        elif dst in relays and src in kept and (src, src) not in first:
            first.append((src, src))
            second.append((src, dst))
        else:
            left.append((src, dst))
    brings = {dst for src, dst in first if src != dst and dst not in relays}
    return first, second, left, brings


def onward(row_devices, col_devices):
    ratio = row_devices // col_devices

    def at(z, y, c):
        return (z * ratio + y) * col_devices + c

    rows = [(z, y) for z in range(col_devices) for y in range(ratio)]
    across, askew = [], []
    for d in range(2, col_devices, 2):
        pairs = [
            (at(z, y, c), at(z, y, c + d), at(z, y, (c + d) ^ 1))
            for z, y in rows
            for c in range(min(z + 1, col_devices - d))
        ]
        swapped = {at(z, y, c) for z, y in rows if z < col_devices // 2 for c in range(col_devices)}
        across.append([(src, other if src in swapped else same) for src, same, other in pairs])
        askew.append([(src, same if src in swapped else other) for src, same, other in pairs])
    beside = [(at(z, y, c), at(z, y, c + 1)) for z, y in rows for c in range(0, min(z + 1, col_devices), 2)]
    along = [(at(z, y, c), at(z, y, c + 1)) for z, y in rows for c in range(0, col_devices, 2)]
    along += [(at(z, y, c + 1), at(z, y, c)) for z, y in rows for c in range(2, col_devices, 2)]
    return across, askew, along, beside


def member(devices, index):
    found = jnp.int32(0)
    for word in range(max(devices, default=0) // 31 + 1):
        bits = sum(1 << (d % 31) for d in devices if d // 31 == word)
        found = found + jnp.where(index // 31 == word, (jnp.int32(bits) >> (index % 31)) & 1, 0)
    return found != 0


def held(shape, dtype):
    return pltpu.VMEM(shape, dtype)


def keep(x):
    return pltpu.with_memory_space_constraint(x, pltpu.VMEM)


def place():
    return lax.axis_index("row"), lax.axis_index("col")


def copies(jobs, sem):
    out = [pltpu.make_async_copy(src, dst, sem.at[i]) for i, (src, dst) in enumerate(jobs)]
    for copy in out:
        copy.start()
    for copy in out:
        copy.wait()


def pack(lesser, greater, spans):
    rows, width = lesser.shape
    ratio = width // rows

    def kernel(less_ref, great_ref, *refs):
        outs, sem = refs[:-1], refs[-1]
        my_row, _ = place()
        jobs = []
        for out, (s, r0, r1, c0, c1) in zip(outs, spans):
            block = lax.rem(my_row + s, ratio)
            start = pl.multiple_of(block * rows + c0, LANES)
            for i, ref in enumerate((less_ref, great_ref)):
                jobs.append((ref.at[pl.ds(r0, r1 - r0), pl.ds(start, c1 - c0)], out.at[i]))
        copies(jobs, sem)

    return pl.pallas_call(
        kernel,
        out_shape=[held((2, r1 - r0, c1 - c0), BF16) for _, r0, r1, c0, c1 in spans],
        in_specs=[pl.BlockSpec(memory_space=pl.ANY)] * 2,
        out_specs=[pl.BlockSpec(memory_space=pltpu.VMEM)] * len(spans),
        scratch_shapes=[pltpu.SemaphoreType.DMA((2 * len(spans),))],
        compiler_params=ROOM,
        name="pack_windows",
    )(*(pltpu.with_memory_space_constraint(x, pltpu.HBM) for x in (lesser, greater)))


def sigmas(lesser, greater, screened_lesser, screened_greater):
    rows, width = lesser.shape
    ratio = width // rows
    steps = 4
    tile = rows // steps

    def kernel(*refs):
        ins, both_ref, bufs, sem = refs[:4], refs[4], refs[5:9], refs[9]
        my_row, my_col = place()
        loads = []
        for i in range(steps):
            at = pl.ds(i * tile, tile)
            loads.append([])
            for n in range(4):
                copy = pltpu.make_async_copy(ins[n].at[at], bufs[n].at[at], sem.at[4 * i + n])
                copy.start()
                loads[i].append(copy)
        for i in range(steps):
            for copy in loads[i]:
                copy.wait()
            at = pl.ds(i * tile, tile)
            for k in range(ratio):
                cols = pl.ds(k * rows, rows)
                less, great, wless, wgreat = (buf[at, cols].astype(F32) for buf in bufs)
                prod_less = less * wless
                later = my_row * rows + i * tile + lax.broadcasted_iota(jnp.int32, (tile, rows), 0)
                inner = my_col * width + k * rows + lax.broadcasted_iota(jnp.int32, (tile, rows), 1)
                both_ref[k, at, :rows] = jnp.where(inner <= later, great * wgreat - prod_less, 0.0).astype(BF16)
                both_ref[k, at, rows:] = prod_less.astype(BF16)

    args = (lesser, greater, screened_lesser, screened_greater)
    return pl.pallas_call(
        kernel,
        out_shape=held((ratio, rows, 2 * rows), BF16),
        in_specs=[pl.BlockSpec(memory_space=pl.ANY)] * 4,
        out_specs=pl.BlockSpec(memory_space=pltpu.VMEM),
        scratch_shapes=[pltpu.VMEM((rows, width), BF16)] * 4 + [pltpu.SemaphoreType.DMA((4 * steps,))],
        compiler_params=ROOM,
        name="sigma_blocks",
    )(*(pltpu.with_memory_space_constraint(x, pltpu.HBM) for x in args))


def block_term(both_ref, k, win, my_row, my_col, rows, width, first):
    green, great = win(0), win(1)
    diff = (green.astype(F32) - great.astype(F32)).astype(BF16)
    inner = my_col * width + k * rows + lax.broadcasted_iota(jnp.int32, diff.shape, 0)
    times = my_row * rows + first + lax.broadcasted_iota(jnp.int32, diff.shape, 1)
    diff = jnp.where(inner <= times, diff, jnp.zeros((), BF16))
    return jnp.dot(both_ref[k], jnp.concatenate([green, diff], axis=0), preferred_element_type=F32)


def partial(both, own, wins, brings, first, width, scale, shifts, before=()):
    ratio, rows, _ = both.shape
    cols = own.shape[-1]
    counts = [len(wins[s]) for s in shifts]
    col_devices = lax.axis_size("col")
    shapes = [held((rows, cols), F32)] + [held((rows, cols), BF16)] * (ratio - 1 in shifts)

    def kernel(both_ref, own_ref, *refs):
        outs = refs[len(refs) - len(shapes) :]
        my_row, my_col = place()
        some = my_col <= my_row // ratio

        @pl.when(some)
        def _():
            total, at = None, len(before)
            for s, count in zip(shifts, counts):
                k = lax.rem(my_row + ratio - s, ratio)
                mine = refs[at : at + count]
                at += count
                valid = member(brings[s], my_row * col_devices + my_col)

                def win(i, s=s, mine=mine, valid=valid):
                    got = jnp.where(valid, mine[0][i], jnp.zeros((), BF16))
                    for ref in mine[1:]:
                        got = got + ref[i]
                    if s == 0:
                        got = jnp.where(my_col == my_row // ratio, own_ref[i], got)
                    return got

                term = block_term(both_ref, k, win, my_row, my_col, rows, width, first)
                total = term if total is None else total + term
            total = scale * total
            if before:
                total = total + refs[0][...]
            for ref in outs:
                ref[...] = total.astype(ref.dtype)

        @pl.when(jnp.logical_not(some))
        def _():
            for ref in outs:
                ref[...] = jnp.zeros(ref.shape, ref.dtype)

    return pl.pallas_call(
        kernel,
        out_shape=shapes,
        in_specs=[pl.BlockSpec(memory_space=pltpu.VMEM)] * (2 + len(before) + sum(counts)),
        out_specs=[pl.BlockSpec(memory_space=pltpu.VMEM)] * len(shapes),
        compiler_params=ROOM,
        name="partial",
    )(*map(keep, [both, own, *before]), *[keep(x) for s in shifts for x in wins[s]])


def chunk_sums(part, got, relayed):
    outs = [held(part.shape, F32)] + ([held(part.shape, BF16)] if relayed else [])

    def kernel(part_ref, *refs):
        _, my_col = place()
        came = jnp.zeros(part_ref.shape, F32)
        for ref in refs[: len(got)]:
            came = came + ref[...].astype(F32)
        total = came + part_ref[...]
        refs[len(got)][...] = total
        if relayed:
            refs[-1][...] = jnp.where(lax.rem(my_col, 2) == 0, total, came).astype(BF16)

    args = [part, *got]
    return pl.pallas_call(
        kernel,
        out_shape=outs,
        in_specs=[pl.BlockSpec(memory_space=pltpu.VMEM)] * len(args),
        out_specs=[pl.BlockSpec(memory_space=pltpu.VMEM)] * len(outs),
        compiler_params=ROOM,
        name="chunk_sums",
    )(*map(keep, args))


def accumulate(totals, came):
    rows, cols = totals[0].shape
    n = len(totals)

    def kernel(*refs):
        for q in range(n):
            refs[-1][:, q * cols : (q + 1) * cols] = refs[q][...] + refs[n + q][...].astype(F32)

    return pl.pallas_call(
        kernel,
        out_shape=jax.ShapeDtypeStruct((rows, n * cols), F32),
        in_specs=[pl.BlockSpec(memory_space=pltpu.VMEM)] * (2 * n),
        out_specs=pl.BlockSpec(memory_space=pltpu.VMEM),
        compiler_params=ROOM,
        name="accumulate",
    )(*map(keep, [*totals, *came]))


def local(lesser, greater, screened_lesser, screened_greater):
    rows, width = lesser.shape
    row_devices, col_devices = lax.axis_size("row"), lax.axis_size("col")
    ratio = row_devices // col_devices
    scale = float(width * col_devices) ** (-0.5)
    across, askew, along, beside = onward(row_devices, col_devices)
    chunks = WINDOW // LANES

    jobs = [(s, q) for q in range(chunks) for s in range(ratio)]
    packed = pack(lesser, greater, [(s, 0, rows, q * LANES, (q + 1) * LANES) for s, q in jobs])
    ready = dict(zip(jobs, packed))
    plan = {job: route(row_devices, col_devices, job[0]) for job in jobs}

    def send(x, pairs):
        return lax.ppermute(x, AXES, pairs)

    hop = {(s, q): send(ready[s, q], plan[s, q][0]) for s, q in jobs}
    both = sigmas(lesser, greater, screened_lesser, screened_greater)
    tie = jobs[-ratio]
    hop[tie], both = lax.optimization_barrier((hop[tie], both))
    wins = {(s, q): [hop[s, q], send(hop[s, q], plan[s, q][1])] for s, q in jobs}
    for s, q in jobs:
        if plan[s, q][2]:
            wins[s, q].append(send(ready[s, q], plan[s, q][2]))
    totals, came = [], []
    for q in range(chunks):
        mine = [wins[s, q] for s in range(ratio)]
        brings = [plan[s, q][3] for s in range(ratio)]
        steps = [range(ratio)] if q < chunks - 1 else [[s] for s in range(ratio)]
        found = ()
        for shifts in steps:
            found = partial(both, ready[0, q], mine, brings, q * LANES, width, scale, shifts, found)
        part, out = found
        if q < chunks - 1:
            total, message = chunk_sums(part, [send(out, pairs) for pairs in across], True)
            came.append(send(message, along))
        else:
            (total,) = chunk_sums(part, [send(out, pairs) for pairs in across + askew], False)
            came.append(send(out, beside))
        totals.append(total)
    return accumulate(totals, came)


def solution(mesh):
    in_specs = (P("row", "col"),) * 4
    return jax.shard_map(local, mesh=mesh, in_specs=in_specs, out_specs=P("row", "col"), check_vma=False)
```

```python
import functools

import jax
import jax.numpy as jnp
from jax import lax
from jax.experimental import pallas as pl
from jax.experimental.pallas import tpu as pltpu
from jax.sharding import PartitionSpec as P

WINDOW = 256
LANES = 128
AXES = ("row", "col")
BF16 = jnp.bfloat16
F32 = jnp.float32
ROOM = pltpu.CompilerParams(vmem_limit_bytes=16 * 2**20)


def route(row_devices, col_devices, s):
    ratio = row_devices // col_devices
    half = col_devices // 2
    straight = col_devices - half // 2

    def at(z, y, g):
        return (z * ratio + y) * col_devices + g

    first, second, left = [], [], []
    near, hops = {}, []
    for z in range(col_devices):
        for y in range(ratio):
            to = (y + s) % ratio
            for g in range(z, col_devices):
                src, dst = at(z, y, g), at(g, to, z)
                if z < half and g >= straight:
                    hops.append((z, y, src, dst))
                elif z < half <= g:
                    first.append((src, dst))
                elif z < g or y < to:
                    near[dst] = src
    relays, kept = set(), set()
    for z, y, src, dst in hops:
        choice = None
        turn = (z + (y + 1) * (s % 2)) % 2
        for g in range(half)[:: -1 if turn else 1]:
            relay = at(z, y, g)
            if relay not in relays and relay not in kept and near.get(relay) not in relays:
                choice = relay
                break
        if choice is None:
            left.append((src, dst))
            continue
        relays.add(choice)
        if choice in near:
            kept.add(near[choice])
        first.append((src, choice))
        second.append((choice, dst))
    for dst, src in near.items():
        if dst not in relays and src not in kept:
            first.append((src, dst))
        elif dst in relays and src in kept and (src, src) not in first:
            first.append((src, src))
            second.append((src, dst))
        else:
            left.append((src, dst))
    brings = {dst for src, dst in first if src != dst and dst not in relays}
    return first, second, left, brings


def onward(row_devices, col_devices):
    ratio = row_devices // col_devices

    def at(z, y, c):
        return (z * ratio + y) * col_devices + c

    rows = [(z, y) for z in range(col_devices) for y in range(ratio)]
    across, askew = [], []
    for d in range(2, col_devices, 2):
        pairs = [
            (at(z, y, c), at(z, y, c + d), at(z, y, (c + d) ^ 1))
            for z, y in rows
            for c in range(min(z + 1, col_devices - d))
        ]
        swapped = {at(z, y, c) for z, y in rows if z < col_devices // 2 for c in range(col_devices)}
        across.append([(src, other if src in swapped else same) for src, same, other in pairs])
        askew.append([(src, same if src in swapped else other) for src, same, other in pairs])
    beside = [(at(z, y, c), at(z, y, c + 1)) for z, y in rows for c in range(0, min(z + 1, col_devices), 2)]
    along = [(at(z, y, c), at(z, y, c + 1)) for z, y in rows for c in range(0, col_devices, 2)]
    along += [(at(z, y, c + 1), at(z, y, c)) for z, y in rows for c in range(2, col_devices, 2)]
    return across, askew, along, beside


def member(devices, index):
    found = jnp.int32(0)
    for word in range(max(devices, default=0) // 31 + 1):
        bits = sum(1 << (d % 31) for d in devices if d // 31 == word)
        found = found + jnp.where(index // 31 == word, (jnp.int32(bits) >> (index % 31)) & 1, 0)
    return found != 0


def held(shape, dtype):
    return pltpu.VMEM(shape, dtype)


def keep(x):
    return pltpu.with_memory_space_constraint(x, pltpu.VMEM)


def place():
    return lax.axis_index("row"), lax.axis_index("col")


def copies(jobs, sem):
    out = [pltpu.make_async_copy(src, dst, sem.at[i]) for i, (src, dst) in enumerate(jobs)]
    for copy in out:
        copy.start()
    for copy in out:
        copy.wait()


def pack(lesser, greater, spans):
    rows, width = lesser.shape
    ratio = width // rows

    def kernel(less_ref, great_ref, *refs):
        outs, sem = refs[:-1], refs[-1]
        my_row, _ = place()
        jobs = []
        for out, (s, r0, r1, c0, c1) in zip(outs, spans):
            block = lax.rem(my_row + s, ratio)
            start = pl.multiple_of(block * rows + c0, LANES)
            for i, ref in enumerate((less_ref, great_ref)):
                jobs.append((ref.at[pl.ds(r0, r1 - r0), pl.ds(start, c1 - c0)], out.at[i]))
        copies(jobs, sem)

    return pl.pallas_call(
        kernel,
        out_shape=[held((2, r1 - r0, c1 - c0), BF16) for _, r0, r1, c0, c1 in spans],
        in_specs=[pl.BlockSpec(memory_space=pl.ANY)] * 2,
        out_specs=[pl.BlockSpec(memory_space=pltpu.VMEM)] * len(spans),
        scratch_shapes=[pltpu.SemaphoreType.DMA((2 * len(spans),))],
        compiler_params=ROOM,
        name="pack_windows",
    )(*(pltpu.with_memory_space_constraint(x, pltpu.HBM) for x in (lesser, greater)))


def sigmas(lesser, greater, screened_lesser, screened_greater):
    rows, width = lesser.shape
    ratio = width // rows
    steps = 4
    tile = rows // steps

    def kernel(*refs):
        ins, both_ref, bufs, sem = refs[:4], refs[4], refs[5:9], refs[9]
        my_row, my_col = place()
        loads = []
        for i in range(steps):
            at = pl.ds(i * tile, tile)
            loads.append([])
            for n in range(4):
                copy = pltpu.make_async_copy(ins[n].at[at], bufs[n].at[at], sem.at[4 * i + n])
                copy.start()
                loads[i].append(copy)
        for i in range(steps):
            for copy in loads[i]:
                copy.wait()
            at = pl.ds(i * tile, tile)
            for k in range(ratio):
                cols = pl.ds(k * rows, rows)
                less, great, wless, wgreat = (buf[at, cols].astype(F32) for buf in bufs)
                prod_less = less * wless
                later = my_row * rows + i * tile + lax.broadcasted_iota(jnp.int32, (tile, rows), 0)
                inner = my_col * width + k * rows + lax.broadcasted_iota(jnp.int32, (tile, rows), 1)
                both_ref[k, at, :rows] = jnp.where(inner <= later, great * wgreat - prod_less, 0.0).astype(BF16)
                both_ref[k, at, rows:] = prod_less.astype(BF16)

    args = (lesser, greater, screened_lesser, screened_greater)
    return pl.pallas_call(
        kernel,
        out_shape=held((ratio, rows, 2 * rows), BF16),
        in_specs=[pl.BlockSpec(memory_space=pl.ANY)] * 4,
        out_specs=pl.BlockSpec(memory_space=pltpu.VMEM),
        scratch_shapes=[pltpu.VMEM((rows, width), BF16)] * 4 + [pltpu.SemaphoreType.DMA((4 * steps,))],
        compiler_params=ROOM,
        name="sigma_blocks",
    )(*(pltpu.with_memory_space_constraint(x, pltpu.HBM) for x in args))


def block_term(both_ref, k, win, my_row, my_col, rows, width, first):
    green, great = win(0), win(1)
    diff = (green.astype(F32) - great.astype(F32)).astype(BF16)
    inner = my_col * width + k * rows + lax.broadcasted_iota(jnp.int32, diff.shape, 0)
    times = my_row * rows + first + lax.broadcasted_iota(jnp.int32, diff.shape, 1)
    diff = jnp.where(inner <= times, diff, jnp.zeros((), BF16))
    return jnp.dot(both_ref[k], jnp.concatenate([green, diff], axis=0), preferred_element_type=F32)


def partial(both, own, wins, brings, first, width, scale, shifts, before=()):
    ratio, rows, _ = both.shape
    cols = own.shape[-1]
    counts = [len(wins[s]) for s in shifts]
    col_devices = lax.axis_size("col")
    shapes = [held((rows, cols), F32)] + [held((rows, cols), BF16)] * (ratio - 1 in shifts)

    def kernel(both_ref, own_ref, *refs):
        outs = refs[len(refs) - len(shapes) :]
        my_row, my_col = place()
        some = my_col <= my_row // ratio

        @pl.when(some)
        def _():
            total, at = None, len(before)
            for s, count in zip(shifts, counts):
                k = lax.rem(my_row + ratio - s, ratio)
                mine = refs[at : at + count]
                at += count
                valid = member(brings[s], my_row * col_devices + my_col)

                def win(i, s=s, mine=mine, valid=valid):
                    got = jnp.where(valid, mine[0][i], jnp.zeros((), BF16))
                    for ref in mine[1:]:
                        got = got + ref[i]
                    if s == 0:
                        got = jnp.where(my_col == my_row // ratio, own_ref[i], got)
                    return got

                term = block_term(both_ref, k, win, my_row, my_col, rows, width, first)
                total = term if total is None else total + term
            total = scale * total
            if before:
                total = total + refs[0][...]
            for ref in outs:
                ref[...] = total.astype(ref.dtype)

        @pl.when(jnp.logical_not(some))
        def _():
            for ref in outs:
                ref[...] = jnp.zeros(ref.shape, ref.dtype)

    return pl.pallas_call(
        kernel,
        out_shape=shapes,
        in_specs=[pl.BlockSpec(memory_space=pltpu.VMEM)] * (2 + len(before) + sum(counts)),
        out_specs=[pl.BlockSpec(memory_space=pltpu.VMEM)] * len(shapes),
        compiler_params=ROOM,
        name="partial",
    )(*map(keep, [both, own, *before]), *[keep(x) for s in shifts for x in wins[s]])


def chunk_sums(part, got, relayed):
    outs = [held(part.shape, F32)] + ([held(part.shape, BF16)] if relayed else [])

    def kernel(part_ref, *refs):
        _, my_col = place()
        came = jnp.zeros(part_ref.shape, F32)
        for ref in refs[: len(got)]:
            came = came + ref[...].astype(F32)
        total = came + part_ref[...]
        refs[len(got)][...] = total
        if relayed:
            refs[-1][...] = jnp.where(lax.rem(my_col, 2) == 0, total, came).astype(BF16)

    args = [part, *got]
    return pl.pallas_call(
        kernel,
        out_shape=outs,
        in_specs=[pl.BlockSpec(memory_space=pltpu.VMEM)] * len(args),
        out_specs=[pl.BlockSpec(memory_space=pltpu.VMEM)] * len(outs),
        compiler_params=ROOM,
        name="chunk_sums",
    )(*map(keep, args))


def accumulate(totals, came):
    rows, cols = totals[0].shape
    n = len(totals)

    def kernel(*refs):
        for q in range(n):
            refs[-1][:, q * cols : (q + 1) * cols] = refs[q][...] + refs[n + q][...].astype(F32)

    return pl.pallas_call(
        kernel,
        out_shape=jax.ShapeDtypeStruct((rows, n * cols), F32),
        in_specs=[pl.BlockSpec(memory_space=pltpu.VMEM)] * (2 * n),
        out_specs=pl.BlockSpec(memory_space=pltpu.VMEM),
        compiler_params=ROOM,
        name="accumulate",
    )(*map(keep, [*totals, *came]))


def local(lesser, greater, screened_lesser, screened_greater):
    rows, width = lesser.shape
    row_devices, col_devices = lax.axis_size("row"), lax.axis_size("col")
    ratio = row_devices // col_devices
    scale = float(width * col_devices) ** (-0.5)
    across, askew, along, beside = onward(row_devices, col_devices)
    chunks = WINDOW // LANES

    jobs = [(s, q) for q in range(chunks) for s in range(ratio)]
    packed = pack(lesser, greater, [(s, 0, rows, q * LANES, (q + 1) * LANES) for s, q in jobs])
    ready = dict(zip(jobs, packed))
    plan = {job: route(row_devices, col_devices, job[0]) for job in jobs}

    def send(x, pairs):
        return lax.ppermute(x, AXES, pairs)

    hop = {(s, q): send(ready[s, q], plan[s, q][0]) for s, q in jobs}
    both = sigmas(lesser, greater, screened_lesser, screened_greater)
    tie = jobs[-ratio]
    hop[tie], both = lax.optimization_barrier((hop[tie], both))
    wins = {(s, q): [hop[s, q], send(hop[s, q], plan[s, q][1])] for s, q in jobs}
    for s, q in jobs:
        if plan[s, q][2]:
            wins[s, q].append(send(ready[s, q], plan[s, q][2]))
    totals, came = [], []
    for q in range(chunks):
        mine = [wins[s, q] for s in range(ratio)]
        brings = [plan[s, q][3] for s in range(ratio)]
        steps = [range(ratio)] if q < chunks - 1 else [[s] for s in range(ratio)]
        found = ()
        for shifts in steps:
            found = partial(both, ready[0, q], mine, brings, q * LANES, width, scale, shifts, found)
        part, out = found
        if q < chunks - 1:
            total, message = chunk_sums(part, [send(out, pairs) for pairs in across], True)
            came.append(send(message, along))
        else:
            (total,) = chunk_sums(part, [send(out, pairs) for pairs in across + askew], False)
            came.append(send(out, beside))
        totals.append(total)
    return accumulate(totals, came)


def solution(mesh):
    in_specs = (P("row", "col"),) * 4
    return jax.shard_map(local, mesh=mesh, in_specs=in_specs, out_specs=P("row", "col"), check_vma=False)
```
